32 devices in a mesh: dp: 4 (over z), row: 4 (over x, core), col: 2 (over y).
Axes of the slice: x: 2, y: 2, z: 4, core: 2. Of those that a mesh axis runs over, the one named last changes fastest.
Arguments:
- activations: bfloat16 [4096, 18432], P(('dp', 'col'), 'row'), may hold values from -6 to 6
- cotangent: bfloat16 [4096, 16384], P(('dp', 'row'), 'col'), may hold values from -0.09375 to 0.09375
- weight: float32 [18432, 16384], P(('row', 'dp'), 'col'), may hold values from -60 to 60
- row_moment: float32 [18432], P(('row', 'dp')), may hold values from 0.05 to 1
- col_moment: float32 [16384], P('col'), may hold values from 0.05 to 1
Outputs:
- new_weight: float32 [18432, 16384], P(('row', 'dp'), 'col')
- clipped_update: bfloat16 [18432, 16384], P(('row', 'dp'), 'col')
- new_row_moment: float32 [18432], P(('row', 'dp'))
- new_col_moment: float32 [16384], P('col')
The draws below stay inside these ranges and needn't reach their ends.
All inputs are finite; a program needn't handle non-finite values.
Results may differ from the reference program's by a relative error of at most 0.001.
Values may be sent and summed in bfloat16 or wider, within the bound.
No kernel may reach another device: no remote copies, remote signals or barrier semaphores. Data moves between devices by JAX's collectives and lax.ppermute only.
A program may use at most 384 MiB of HBM per device.

```python
import math
import jax
import jax.numpy as jnp
from jax import lax

D = 18432
F = 16384
STEP = 10
TOKENS = 4096


def draw_weight(key, part):
    key = jax.random.fold_in(key, 7)
    key_rows, key_cols, key_base = jax.random.split(key, 3)
    position = jnp.arange(D, dtype=jnp.float32) / D
    row_factor = 3.0 ** (position - 0.5) * 10.0 ** jax.random.uniform(key_rows, (D,), jnp.float32, -0.5, 0.5)
    col_factor = 10.0 ** jax.random.uniform(key_cols, (F,), jnp.float32, -0.25, 0.25)
    base_values = jnp.clip(jax.random.normal(key_base, (D, F), jnp.float32), -6.0, 6.0)
    return (base_values * row_factor[:, None] * col_factor[None, :]).astype(jnp.float32)


def spiked(result, stream_key, source, target, parts, factor):
    def block_of(dim):
        return (jnp.arange(result.shape[dim]) // (result.shape[dim] // parts)).reshape((-1,) + (1,) * (result.ndim - 1 - dim))

    first = jax.random.permutation(stream_key, parts)[block_of(target)]
    other_side = (block_of(target) + parts // 2) % parts
    return jnp.where((block_of(source) == first) | (block_of(source) == other_side), factor * result, result)


def levels(stream_key, shape, pieces, smallest, high):
    loudness = 1.0
    for dim, blocks in pieces:
        draws = jax.random.uniform(jax.random.fold_in(jax.random.fold_in(stream_key, 6), dim), (blocks,), jnp.float32, smallest / len(pieces), high / len(pieces))
        loudness = loudness * jnp.repeat(jnp.exp(draws), shape[dim] // blocks).reshape((-1,) + (1,) * (len(shape) - 1 - dim))
    return loudness


def noise(stream_key, dims, scale, limit, shards=(), held_as=jnp.bfloat16):
    gain = levels(stream_key, dims, shards, -0.22, 0.18) if shards else 1.0
    entries = jax.random.normal(stream_key, dims, jnp.float32) * scale * gain
    return jnp.minimum(jnp.maximum(entries, -limit), limit).astype(held_as)


def gaussian_with(own_key, extent, deviation, limit, cuts, heavy, kind=jnp.bfloat16):
    drawn = deviation * jax.random.normal(own_key, extent, jnp.float32)
    if cuts:
        drawn = drawn * levels(own_key, extent, cuts, -0.22, 0.18)
    return jnp.clip(spiked(drawn, jax.random.fold_in(own_key, 3), *heavy), -limit, limit).astype(kind)


def setup_inputs(seed: int = 0) -> dict:
    key_list = jax.random.split(jax.random.key(seed), 6)
    return {
        "activations": gaussian_with(key_list[0], (TOKENS, D), 1.0, 6.0, ((0, 8), (1, 4)), (0, 1, 8, 2.0)),
        "cotangent": noise(key_list[1], (TOKENS, F), TOKENS ** -0.5, 0.09375, ((0, 16), (1, 2))),
        "weight": draw_weight(jax.random.fold_in(key_list[5], 71), 0),
        "row_moment": jnp.clip(jnp.exp(math.log(1.0) - 2.9957323 * jax.random.uniform(key_list[3], (D,), jnp.float32) ** levels(key_list[3], (D,), ((0, 16),), -0.2, 0.2)), 0.05, 1.0),
        "col_moment": jnp.clip(jnp.exp(math.log(1.0) - 2.9957323 * jax.random.uniform(key_list[4], (F,), jnp.float32) ** levels(key_list[4], (F,), ((0, 2),), -0.2, 0.2)), 0.05, 1.0),
    }


def reference(activations, cotangent, weight, row_moment, col_moment):
    decay_rate = 1.0 - float(STEP) ** (-0.8)
    relative = min(0.01, float(STEP) ** (-0.5))
    gradient = jnp.dot(activations.T, cotangent, preferred_element_type=jnp.float32)
    squared = gradient * gradient
    row_new = decay_rate * row_moment + (1.0 - decay_rate) * lax.optimization_barrier(jnp.sum(squared, axis=1)) / F
    col_new = decay_rate * col_moment + (1.0 - decay_rate) * lax.optimization_barrier(jnp.sum(squared, axis=0)) / D
    update = gradient * lax.rsqrt(row_new)[:, None] * lax.rsqrt(col_new)[None, :]
    clip_factor = jnp.maximum(1.0, jnp.sqrt(jnp.sum(update * update) / (D * F)))
    clipped = update / clip_factor
    new_weight = weight - relative * clipped
    return (new_weight, clipped.astype(jnp.bfloat16), row_new, col_new)
```

```python
import functools

import jax
import jax.numpy as jnp
from jax import lax
from jax.experimental import pallas as pl
from jax.experimental.pallas import tpu as pltpu
from jax.sharding import PartitionSpec as P

D = 18432
F = 16384
STEP = 10
CHUNKS = 8


def product_kernel(count, act_ref, *refs):
    blocks, (grad_ref, row_ref, col_ref, held) = refs[:count], refs[count:]
    depth = blocks[0].shape[0]
    for k, block in enumerate(blocks):
        held[k * depth : (k + 1) * depth, :] = block[...]
    grad = jnp.dot(act_ref[...], held[...], preferred_element_type=jnp.float32)
    grad_ref[...] = grad
    squared = grad * grad
    col_ref[...] = jnp.sum(squared, axis=0, keepdims=True)
    lanes = squared[:, :128]
    for at in range(128, squared.shape[1], 128):
        lanes = lanes + squared[:, at : at + 128]

    @pl.when(pl.program_id(0) == 0)
    def _():
        row_ref[...] = jnp.zeros_like(row_ref)

    row_ref[...] += lanes


def product(act, blocks):
    rows, tokens = act.shape
    depth, width = blocks[0].shape
    tile = min(256, width)
    return pl.pallas_call(
        functools.partial(product_kernel, len(blocks)),
        grid=(width // tile,),
        in_specs=[pl.BlockSpec((rows, tokens), lambda j: (0, 0))]
        + [pl.BlockSpec((depth, tile), lambda j: (0, j)) for _ in blocks],
        out_specs=[
            pl.BlockSpec((rows, tile), lambda j: (0, j)),
            pl.BlockSpec((rows, 128), lambda j: (0, 0)),
            pl.BlockSpec((1, tile), lambda j: (0, j)),
        ],
        out_shape=[
            jax.ShapeDtypeStruct((rows, width), jnp.float32),
            jax.ShapeDtypeStruct((rows, 128), jnp.float32),
            jax.ShapeDtypeStruct((1, width), jnp.float32),
        ],
        scratch_shapes=[pltpu.VMEM((tokens, tile), jnp.bfloat16)],
        cost_estimate=pl.CostEstimate(
            flops=2 * rows * tokens * width,
            bytes_accessed=2 * (rows + width) * tokens + 4 * rows * width,
            transcendentals=0,
        ),
        compiler_params=pltpu.CompilerParams(vmem_limit_bytes=48 * 2**20),
        name="product",
    )(act, *blocks)


def step_kernel(count, relative, clip_ref, row_ref, col_ref, weight_ref, *refs):
    grads, (new_ref, clipped_ref) = refs[:count], refs[count:]
    for k in range(count):

        @pl.when(pl.program_id(0) == k)
        def _(grad_ref=grads[k]):
            clipped = grad_ref[...] * (row_ref[...] * clip_ref[0, 0]) * col_ref[...]
            new_ref[...] = weight_ref[...] - relative * clipped
            clipped_ref[...] = clipped.astype(jnp.bfloat16)


def weight_step(relative, inverse_clip, row_scale, col_scale, weight, grads):
    rows, columns = weight.shape
    width = grads[0].shape[1]
    count = len(grads)
    tile = 128
    steps = rows // tile

    def own(k):
        return lambda c, i: (jnp.where(c == k, i, jnp.where(c < k, 0, steps - 1)), 0)

    return pl.pallas_call(
        functools.partial(step_kernel, count, relative),
        grid=(count, steps),
        in_specs=[
            pl.BlockSpec(memory_space=pltpu.SMEM),
            pl.BlockSpec((tile, 1), lambda c, i: (i, 0)),
            pl.BlockSpec((1, width), lambda c, i: (0, c)),
            pl.BlockSpec((tile, width), lambda c, i: (i, c)),
        ]
        + [pl.BlockSpec((tile, width), own(k)) for k in range(count)],
        out_specs=[
            pl.BlockSpec((tile, width), lambda c, i: (i, c)),
            pl.BlockSpec((tile, width), lambda c, i: (i, c)),
        ],
        out_shape=[
            jax.ShapeDtypeStruct((rows, columns), jnp.float32),
            jax.ShapeDtypeStruct((rows, columns), jnp.bfloat16),
        ],
        cost_estimate=pl.CostEstimate(
            flops=5 * rows * columns, bytes_accessed=14 * rows * columns, transcendentals=0
        ),
        compiler_params=pltpu.CompilerParams(vmem_limit_bytes=48 * 2**20),
        name="weight_step",
    )(inverse_clip.reshape(1, 1), row_scale[:, None], col_scale[None, :], weight, *grads)


def shifted(value, axis, size, by):
    return lax.ppermute(value, axis, [(i, (i + by) % size) for i in range(size)])


def flipped(value, axis, size, bit):
    return lax.ppermute(value, axis, [(i, i ^ bit) for i in range(size)])


def total(value, axis, size):
    if size & (size - 1):
        return lax.psum(value, axis)
    bit = 1
    while bit < size:
        value = value + flipped(value, axis, size, bit)
        bit *= 2
    return value


def body(sizes, activations, cotangent, weight, row_moment, col_moment):
    n_dp, n_row, n_col = sizes
    z, r, y = lax.axis_index("dp"), lax.axis_index("row"), lax.axis_index("col")
    decay_rate = 1.0 - float(STEP) ** (-0.8)
    relative = min(0.01, float(STEP) ** (-0.5))
    rows = weight.shape[0]
    depth, columns = cotangent.shape
    width = columns // CHUNKS

    held = []
    for s in range(n_dp):
        to = lax.rem(z + s, n_dp)
        piece = lax.dynamic_slice_in_dim(activations, to * rows, rows, axis=1)
        held.append(shifted(piece, "dp", n_dp, s) if s else piece)
    act = []
    for piece in held:
        parts = jnp.zeros((n_col,) + piece.shape, piece.dtype)
        for t in range(n_col):
            part = shifted(piece, "col", n_col, t) if t else piece
            parts = lax.dynamic_update_index_in_dim(parts, part, lax.rem(y - t + n_col, n_col), 0)
        parts = parts.reshape(n_row, depth, rows)
        for u in range(n_row // 2):
            for v in range(2):
                at = lax.rem(r - 2 * u + n_row, n_row) ^ v
                act.append(lax.dynamic_index_in_dim(parts, at, 0, keepdims=False))
    act = jnp.concatenate(act, axis=0).T

    grads, row_lanes, col_new, weighted = [], 0.0, [], 0.0
    for k in range(CHUNKS):
        block = cotangent[:, k * width : (k + 1) * width]
        blocks = []
        for s in range(n_dp):
            if s:
                block = shifted(block, "dp", n_dp, 1)
            for u in range(n_row // 2):
                across = shifted(block, "row", n_row, 2 * u) if u else block
                blocks += [across, flipped(across, "row", n_row, 1)]
        grad, row_part, col_part = product(act, blocks)
        col_sum = total(total(col_part[0], "row", n_row), "dp", n_dp)
        moment = decay_rate * col_moment[k * width : (k + 1) * width] + (1.0 - decay_rate) * col_sum / D
        grads.append(grad)
        row_lanes = row_lanes + row_part
        col_new.append(moment)
        weighted = weighted + jnp.sum(grad * grad * (1.0 / moment)[None, :], axis=1)
    row_sum = jnp.sum(row_lanes, axis=1)
    row_sum, weighted = total(jnp.stack([row_sum, weighted]), "col", n_col)
    row_new = decay_rate * row_moment + (1.0 - decay_rate) * row_sum / F
    col_new = jnp.concatenate(col_new)
    update_total = jnp.sum(weighted / row_new).reshape(1, 1)
    update_total = total(total(update_total, "row", n_row), "dp", n_dp)[0, 0]
    clip_factor = jnp.maximum(1.0, jnp.sqrt(update_total / (D * F)))
    new_weight, clipped = weight_step(
        relative, 1.0 / clip_factor, lax.rsqrt(row_new), lax.rsqrt(col_new), weight, grads
    )
    return (new_weight, clipped, row_new, col_new)


def solution(mesh):
    placed = (
        P(("dp", "col"), "row"),
        P(("dp", "row"), "col"),
        P(("row", "dp"), "col"),
        P(("row", "dp")),
        P("col"),
    )
    sizes = (mesh.shape["dp"], mesh.shape["row"], mesh.shape["col"])
    return jax.shard_map(
        functools.partial(body, sizes),
        mesh=mesh,
        in_specs=placed,
        out_specs=(P(("row", "dp"), "col"), P(("row", "dp"), "col"), P(("row", "dp")), P("col")),
        check_vma=False,
    )
```

```python
import functools

import jax
import jax.numpy as jnp
from jax import lax
from jax.experimental import pallas as pl
from jax.experimental.pallas import tpu as pltpu
from jax.sharding import PartitionSpec as P

D = 18432
F = 16384
STEP = 10
SHARES = (4, 4, 4, 4)
LAST_SHARES = (4, 4, 4, 2, 1, 1)


def product_kernel(count, adds, place_ref, act_ref, *refs):
    blocks, (grad_ref, col_ref, *row_ref, held) = refs[:count], refs[-4 if adds else -3 :]
    depth = blocks[0].shape[0]
    for k, block in enumerate(blocks):
        held[pl.ds(pl.multiple_of(place_ref[k] * depth, depth), depth), :] = block[...]
    grad = jnp.dot(act_ref[...], held[...], preferred_element_type=jnp.float32)
    if not adds:
        grad_ref[...] = grad
        col_ref[...] = grad[:1, :]
        return
    grad = grad + refs[count][...]
    grad_ref[...] = grad
    squared = grad * grad
    col_ref[...] = jnp.sum(squared, axis=0, keepdims=True)
    lanes = squared[:, :128]
    for at in range(128, squared.shape[1], 128):
        lanes = lanes + squared[:, at : at + 128]

    @pl.when(pl.program_id(0) == 0)
    def _():
        row_ref[0][...] = jnp.zeros_like(row_ref[0])

    row_ref[0][...] += lanes


def product(act, half, places, blocks, start, width, grad, columns):
    rows, tokens = act.shape[0], act.shape[1] // 2
    blocks, origins = zip(*blocks)
    depth = blocks[0].shape[0]
    tile = next(t for t in (512, 256, 128) if width % t == 0 and start % t == 0)
    first = start // tile
    adds = half == 1
    before = [] if grad is None else [grad]
    in_place = pl.BlockSpec((rows, tile), lambda j, _: (0, first + j))
    return pl.pallas_call(
        functools.partial(product_kernel, len(blocks), adds),
        grid_spec=pltpu.PrefetchScalarGridSpec(
            num_scalar_prefetch=1,
            grid=(width // tile,),
            in_specs=[pl.BlockSpec((rows, tokens), lambda j, _: (0, half))]
            + [
                pl.BlockSpec((depth, tile), lambda j, _, at=(start - origin) // tile: (0, at + j))
                for origin in origins
            ]
            + [in_place if adds else pl.BlockSpec(memory_space=pl.ANY)] * len(before),
            out_specs=[in_place, pl.BlockSpec((1, tile), lambda j, _: (0, j))]
            + ([pl.BlockSpec((rows, 128), lambda j, _: (0, 0))] if adds else []),
            scratch_shapes=[pltpu.VMEM((tokens, tile), jnp.bfloat16)],
        ),
        out_shape=[
            jax.ShapeDtypeStruct((rows, columns), jnp.float32),
            jax.ShapeDtypeStruct((1, width), jnp.float32),
        ]
        + ([jax.ShapeDtypeStruct((rows, 128), jnp.float32)] if adds else []),
        input_output_aliases={len(blocks) + 2: 0} if before else {},
        cost_estimate=pl.CostEstimate(
            flops=2 * rows * tokens * width,
            bytes_accessed=2 * (rows + width) * tokens + 4 * (2 if adds else 1) * rows * width,
            transcendentals=0,
        ),
        compiler_params=pltpu.CompilerParams(vmem_limit_bytes=44 * 2**20),
        name="product",
    )(places, act, *blocks, *before)


def step_kernel(relative, clip_ref, row_ref, col_ref, weight_ref, grad_ref, new_ref, clipped_ref):
    clipped = grad_ref[...] * (row_ref[...] * clip_ref[0, 0]) * col_ref[...]
    new_ref[...] = weight_ref[...] - relative * clipped
    clipped_ref[...] = clipped.astype(jnp.bfloat16)


def weight_step(relative, inverse_clip, row_scale, col_scale, weight, grad):
    rows, columns = weight.shape
    tile = next(t for t in (64, 32, 16) if rows % t == 0)
    block = pl.BlockSpec((tile, columns), lambda i: (i, 0))
    return pl.pallas_call(
        functools.partial(step_kernel, relative),
        grid=(rows // tile,),
        in_specs=[
            pl.BlockSpec(memory_space=pltpu.SMEM),
            pl.BlockSpec((tile, 1), lambda i: (i, 0)),
            pl.BlockSpec((1, columns), lambda i: (0, 0)),
            block,
            block,
        ],
        out_specs=[block, block],
        out_shape=[
            jax.ShapeDtypeStruct((rows, columns), jnp.float32),
            jax.ShapeDtypeStruct((rows, columns), jnp.bfloat16),
        ],
        cost_estimate=pl.CostEstimate(
            flops=5 * rows * columns, bytes_accessed=14 * rows * columns, transcendentals=0
        ),
        compiler_params=pltpu.CompilerParams(vmem_limit_bytes=40 * 2**20),
        name="weight_step",
    )(inverse_clip.reshape(1, 1), row_scale[:, None], col_scale[None, :], weight, grad)


class Lane:
    def __init__(self, axis, size, ahead):
        self.axis, self.size, self.ahead, self.sent = axis, size, ahead, []

    def send(self, value, target, after=()):
        value = lax.optimization_barrier((value, *after))[0] if after else value
        if len(self.sent) >= self.ahead:
            value, _ = lax.optimization_barrier((value, self.sent[-self.ahead]))
        value = lax.ppermute(value, self.axis, [(i, target(i)) for i in range(self.size)])
        self.sent.append(value)
        return value

    def shift(self, value, by, after=()):
        return self.send(value, lambda i: (i + by) % self.size, after)

    def flip(self, value, bit):
        return self.send(value, lambda i: i ^ bit)


def total(value, axis, size):
    if size & (size - 1):
        return lax.psum(value, axis)
    bit = 1
    while bit < size:
        value = value + lax.ppermute(value, axis, [(i, i ^ bit) for i in range(size)])
        bit *= 2
    return value


def body(sizes, activations, cotangent, weight, row_moment, col_moment):
    n_dp, n_row, n_col = sizes
    n_x = n_row // 2
    z, r, y = lax.axis_index("dp"), lax.axis_index("row"), lax.axis_index("col")
    decay_rate = 1.0 - float(STEP) ** (-0.8)
    relative = min(0.01, float(STEP) ** (-0.5))
    rows = weight.shape[0]
    columns = cotangent.shape[1]
    along_z, along_x, along_y, cores = Lane("dp", n_dp, 2), Lane("row", n_row, 2), Lane("col", n_col, 2), Lane("row", n_row, 4)

    def over_rows(value):
        return total(total(value, "row", n_row), "dp", n_dp)

    own = []
    for u in range(n_x):
        across = along_x.shift(cotangent, 2 * u) if u else cotangent
        own += [across, cores.flip(across, 1)]

    pieces = []
    for s in range(n_dp):
        to = lax.rem(z + s, n_dp)
        piece = lax.dynamic_slice_in_dim(activations, to * rows, rows, axis=1)
        pieces.append(along_z.shift(piece, s) if s else piece)
    act = []
    for piece in pieces:
        parts = [along_y.shift(piece, t) if t else piece for t in range(n_col)]
        ordered = [parts[0]] * n_col
        for at in range(n_col):
            for t in range(1, n_col):
                ordered[at] = jnp.where(lax.rem(y - t + n_col, n_col) == at, parts[t], ordered[at])
        act += ordered
    act = jnp.concatenate(act, axis=0).T
    half = n_dp // 2
    places = jnp.stack(
        [
            n_row * s + (lax.rem(r - 2 * u + n_row, n_row) ^ v)
            for s in range(half)
            for u in range(n_x)
            for v in range(2)
        ]
    ).astype(jnp.int32)

    def cut(shares):
        widths = [columns * share // sum(shares) for share in shares]
        return [(sum(widths[:k]), width) for k, width in enumerate(widths)]

    moving = [(start, cotangent[:, start : start + width]) for start, width in cut(SHARES)]
    first_half, second_half = [(block, 0) for block in own], []
    grad, row_lanes, weighted, col_new = None, 0.0, 0.0, []
    first_done, col_sums, lasts = [], [], cut(LAST_SHARES)
    starts = [start for start, _ in lasts]
    count = 0
    for s in range(1, n_dp):
        last = s == n_dp - 1
        if last:
            holders = [max(k for k, (start, _) in enumerate(moving) if start <= at) for at in starts]
            moving = [
                (at, moving[k][1][:, at - moving[k][0] : at - moving[k][0] + width])
                for k, (at, width) in zip(holders, lasts)
            ]
        for k, (start, block) in enumerate(moving):
            width = block.shape[1]
            after = ()
            if s >= half:
                after = (first_done[count - 2],) if 0 <= count - 2 < len(first_done) else (act,) if count == 0 else ()
                count += 1
            block = along_z.shift(block, 1, after)
            moving[k] = (start, block)
            arrived = []
            for u in range(n_x):
                after = (col_sums[k - 3],) if last and u and k >= 3 else ()
                across = along_x.shift(block, 2 * u, after) if u else block
                arrived += [(across, start), (cores.flip(across, 1), start)]
            if s < half:
                first_half_here = first_half + arrived
                grad, token = product(act, 0, places, first_half_here, start, width, grad, columns)
                first_done.append(token)
            elif not last:
                second_half.append((start, width, arrived))
            else:
                earlier = [b for at, size, blocks in second_half if at <= start < at + size for b in blocks]
                grad, col_part, row_part = product(act, 1, places, earlier + arrived, start, width, grad, columns)
                row_lanes = row_lanes + row_part
                col_sums.append(col_part)
            if last and (k == 1 or k == 3):
                low, high = starts[k - 1], start + width
                col_sum = jnp.concatenate(col_sums[k - 1 : k + 1], axis=1)
                col_new.append(
                    decay_rate * col_moment[low:high] + (1.0 - decay_rate) * over_rows(col_sum)[0] / D
                )
                squared = jnp.square(grad[:, low:high])
                weighted = weighted + jnp.sum(squared * (1.0 / col_new[-1])[None, :], axis=1)
                grad, weighted = lax.optimization_barrier((grad, weighted))
    low, high = starts[4], columns
    col_sum = jnp.concatenate(col_sums[4:], axis=1)
    squared = jnp.square(grad[:, low:high])
    held = decay_rate * col_moment[low:high]
    row_new = decay_rate * row_moment + (1.0 - decay_rate) * total(jnp.sum(row_lanes, axis=1), "col", n_col) / F
    by_row = jnp.full((1, 128), jnp.sum(weighted / row_new) / 128)
    by_col = jnp.sum(squared * (1.0 / row_new)[:, None], axis=0, keepdims=True)
    sums = over_rows(jnp.concatenate([col_sum, by_col, by_row], axis=1))[0]
    count = high - low
    col_new.append(held + (1.0 - decay_rate) * sums[:count] / D)
    update_total = jnp.sum(sums[count : 2 * count] / col_new[-1]) + jnp.sum(sums[2 * count :])
    update_total = total(update_total.reshape(1, 1), "col", n_col)[0, 0]
    col_new = jnp.concatenate(col_new)
    clip_factor = jnp.maximum(1.0, jnp.sqrt(update_total / (D * F)))
    new_weight, clipped = weight_step(
        relative, 1.0 / clip_factor, lax.rsqrt(row_new), lax.rsqrt(col_new), weight, grad
    )
    return (new_weight, clipped, row_new, col_new)


def solution(mesh):
    placed = (
        P(("dp", "col"), "row"),
        P(("dp", "row"), "col"),
        P(("row", "dp"), "col"),
        P(("row", "dp")),
        P("col"),
    )
    sizes = (mesh.shape["dp"], mesh.shape["row"], mesh.shape["col"])
    return jax.shard_map(
        functools.partial(body, sizes),
        mesh=mesh,
        in_specs=placed,
        out_specs=(P(("row", "dp"), "col"), P(("row", "dp"), "col"), P(("row", "dp")), P("col")),
        check_vma=False,
    )
```

```python
import functools

import jax
import jax.numpy as jnp
from jax import lax
from jax.experimental import pallas as pl
from jax.experimental.pallas import tpu as pltpu
from jax.sharding import PartitionSpec as P

D = 18432
F = 16384
STEP = 10
SHARES = (4, 4, 4, 4)
LAST_SHARES = (4, 4, 4, 2, 1, 1)


def product_kernel(count, adds, place_ref, act_ref, *refs):
    blocks, (grad_ref, col_ref, *row_ref, held) = refs[:count], refs[-4 if adds else -3 :]
    depth = blocks[0].shape[0]
    for k, block in enumerate(blocks):
        held[pl.ds(pl.multiple_of(place_ref[k] * depth, depth), depth), :] = block[...]
    grad = jnp.dot(act_ref[...], held[...], preferred_element_type=jnp.float32)
    if not adds:
        grad_ref[...] = grad
        col_ref[...] = grad[:1, :]
        return
    grad = grad + refs[count][...]
    grad_ref[...] = grad
    squared = grad * grad
    col_ref[...] = jnp.sum(squared, axis=0, keepdims=True)
    lanes = squared[:, :128]
    for at in range(128, squared.shape[1], 128):
        lanes = lanes + squared[:, at : at + 128]

    @pl.when(pl.program_id(0) == 0)
    def _():
        row_ref[0][...] = jnp.zeros_like(row_ref[0])

    row_ref[0][...] += lanes


def product(act, half, places, blocks, start, width, grad, columns):
    rows, tokens = act.shape[0], act.shape[1] // 2
    blocks, origins = zip(*blocks)
    depth = blocks[0].shape[0]
    tile = next(t for t in (512, 256, 128) if width % t == 0 and start % t == 0)
    first = start // tile
    adds = half == 1
    before = [] if grad is None else [grad]
    in_place = pl.BlockSpec((rows, tile), lambda j, _: (0, first + j))
    return pl.pallas_call(
        functools.partial(product_kernel, len(blocks), adds),
        grid_spec=pltpu.PrefetchScalarGridSpec(
            num_scalar_prefetch=1,
            grid=(width // tile,),
            in_specs=[pl.BlockSpec((rows, tokens), lambda j, _: (0, half))]
            + [
                pl.BlockSpec((depth, tile), lambda j, _, at=(start - origin) // tile: (0, at + j))
                for origin in origins
            ]
            + [in_place if adds else pl.BlockSpec(memory_space=pl.ANY)] * len(before),
            out_specs=[in_place, pl.BlockSpec((1, tile), lambda j, _: (0, j))]
            + ([pl.BlockSpec((rows, 128), lambda j, _: (0, 0))] if adds else []),
            scratch_shapes=[pltpu.VMEM((tokens, tile), jnp.bfloat16)],
        ),
        out_shape=[
            jax.ShapeDtypeStruct((rows, columns), jnp.float32),
            jax.ShapeDtypeStruct((1, width), jnp.float32),
        ]
        + ([jax.ShapeDtypeStruct((rows, 128), jnp.float32)] if adds else []),
        input_output_aliases={len(blocks) + 2: 0} if before else {},
        cost_estimate=pl.CostEstimate(
            flops=2 * rows * tokens * width,
            bytes_accessed=2 * (rows + width) * tokens + 4 * (2 if adds else 1) * rows * width,
            transcendentals=0,
        ),
        compiler_params=pltpu.CompilerParams(vmem_limit_bytes=44 * 2**20),
        name="product",
    )(places, act, *blocks, *before)


def step_kernel(relative, clip_ref, row_ref, col_ref, weight_ref, grad_ref, new_ref, clipped_ref):
    clipped = grad_ref[...] * (row_ref[...] * clip_ref[0, 0]) * col_ref[...]
    new_ref[...] = weight_ref[...] - relative * clipped
    clipped_ref[...] = clipped.astype(jnp.bfloat16)


def weight_step(relative, inverse_clip, row_scale, col_scale, weight, grad):
    rows, columns = weight.shape
    tile = next(t for t in (64, 32, 16) if rows % t == 0)
    block = pl.BlockSpec((tile, columns), lambda i: (i, 0))
    return pl.pallas_call(
        functools.partial(step_kernel, relative),
        grid=(rows // tile,),
        in_specs=[
            pl.BlockSpec(memory_space=pltpu.SMEM),
            pl.BlockSpec((tile, 1), lambda i: (i, 0)),
            pl.BlockSpec((1, columns), lambda i: (0, 0)),
            block,
            block,
        ],
        out_specs=[block, block],
        out_shape=[
            jax.ShapeDtypeStruct((rows, columns), jnp.float32),
            jax.ShapeDtypeStruct((rows, columns), jnp.bfloat16),
        ],
        cost_estimate=pl.CostEstimate(
            flops=5 * rows * columns, bytes_accessed=14 * rows * columns, transcendentals=0
        ),
        compiler_params=pltpu.CompilerParams(vmem_limit_bytes=40 * 2**20),
        name="weight_step",
    )(inverse_clip.reshape(1, 1), row_scale[:, None], col_scale[None, :], weight, grad)


def shifted(value, axis, size, by):
    return lax.ppermute(value, axis, [(i, (i + by) % size) for i in range(size)])


def flipped(value, axis, size):
    return lax.ppermute(value, axis, [(i, i ^ 1) for i in range(size)])


def total(value, axis, size):
    if size & (size - 1):
        return lax.psum(value, axis)
    bit = 1
    while bit < size:
        value = value + lax.ppermute(value, axis, [(i, i ^ bit) for i in range(size)])
        bit *= 2
    return value


def body(sizes, activations, cotangent, weight, row_moment, col_moment):
    n_dp, n_row, n_col = sizes
    n_x = n_row // 2
    z, r, y = lax.axis_index("dp"), lax.axis_index("row"), lax.axis_index("col")
    decay_rate = 1.0 - float(STEP) ** (-0.8)
    relative = min(0.01, float(STEP) ** (-0.5))
    rows = weight.shape[0]
    columns = cotangent.shape[1]

    def over_rows(value):
        return total(total(value, "row", n_row), "dp", n_dp)

    own = []
    for u in range(n_x):
        across = shifted(cotangent, "row", n_row, 2 * u) if u else cotangent
        own += [across, flipped(across, "row", n_row)]

    pieces = []
    for s in range(n_dp):
        to = lax.rem(z + s, n_dp)
        piece = lax.dynamic_slice_in_dim(activations, to * rows, rows, axis=1)
        pieces.append(shifted(piece, "dp", n_dp, s) if s else piece)
    act = []
    for piece in pieces:
        parts = [shifted(piece, "col", n_col, t) if t else piece for t in range(n_col)]
        ordered = [parts[0]] * n_col
        for at in range(n_col):
            for t in range(1, n_col):
                ordered[at] = jnp.where(lax.rem(y - t + n_col, n_col) == at, parts[t], ordered[at])
        act += ordered
    act = jnp.concatenate(act, axis=0).T
    half = n_dp // 2
    places = jnp.stack(
        [
            n_row * s + (lax.rem(r - 2 * u + n_row, n_row) ^ v)
            for s in range(half)
            for u in range(n_x)
            for v in range(2)
        ]
    ).astype(jnp.int32)

    def cut(shares):
        widths = [columns * share // sum(shares) for share in shares]
        return [(sum(widths[:k]), width) for k, width in enumerate(widths)]

    moving = [(start, cotangent[:, start : start + width]) for start, width in cut(SHARES)]
    first_half = [(block, 0) for block in own]
    grad, row_lanes, weighted, col_new, col_sums = None, 0.0, 0.0, [], []
    lasts = cut(LAST_SHARES)
    starts = [start for start, _ in lasts]

    def finish(k, act, grad):
        nonlocal row_lanes, weighted
        start, width = lasts[k]
        blocks = [
            block
            for s, at, size, held, _ in arrivals
            if s >= half and at <= start < at + size
            for block in held
        ]
        grad, col_part, row_part = product(act, 1, places, blocks, start, width, grad, columns)
        row_lanes = row_lanes + row_part
        col_sums.append(col_part)
        if k in (1, 3):
            low, high = starts[k - 1], start + width
            col_sum = jnp.concatenate(col_sums[k - 1 : k + 1], axis=1)
            col_new.append(decay_rate * col_moment[low:high] + (1.0 - decay_rate) * over_rows(col_sum)[0] / D)
            squared = jnp.square(grad[:, low:high])
            weighted = weighted + jnp.sum(squared * (1.0 / col_new[-1])[None, :], axis=1)
            grad, weighted = lax.optimization_barrier((grad, weighted))
        return grad

    arrivals = []
    settled = 0

    def settle(tied):
        nonlocal settled
        _, start, _, blocks, crossed = arrivals[settled]
        settled += 1
        if crossed and tied is not None:
            tied, *crossed = lax.optimization_barrier((tied, *crossed))
        for across in crossed:
            blocks += [(across, start), (flipped(across, "row", n_row), start)]
        return tied

    for s in range(1, n_dp):
        last = s == n_dp - 1
        if last:
            holders = [max(k for k, (start, _) in enumerate(moving) if start <= at) for at in starts]
            moving = [
                (at, moving[k][1][:, at - moving[k][0] : at - moving[k][0] + width])
                for k, (at, width) in zip(holders, lasts)
            ]
        for k, (start, block) in enumerate(moving):
            at = len(arrivals)
            if at >= 3:
                block = settle(block)
            count = at - len(SHARES) * (half - 1)
            if 2 <= count < 2 + len(SHARES):
                _, first, width, blocks, _ = arrivals[len(SHARES) * (half - 2) + count - 2]
                grad = product(act, 0, places, first_half + blocks, first, width, grad, columns)[0]
                block, grad = lax.optimization_barrier((block, grad))
            block = shifted(block, "dp", n_dp, 1)
            moving[k] = (start, block)
            if last and k >= 3:
                grad = finish(k - 3, act, grad)
                block, grad = lax.optimization_barrier((block, grad))
            blocks = [(block, start), (flipped(block, "row", n_row), start)]
            crossed = [shifted(block, "row", n_row, 2 * u) for u in range(1, n_x)]
            arrivals.append((s, start, block.shape[1], blocks, crossed))
    while settled < len(arrivals):
        settle(None)
    for k in range(len(lasts) - 3, len(lasts)):
        grad = finish(k, act, grad)
    low, high = starts[4], columns
    col_sum = jnp.concatenate(col_sums[4:], axis=1)
    squared = jnp.square(grad[:, low:high])
    held = decay_rate * col_moment[low:high]
    row_new = decay_rate * row_moment + (1.0 - decay_rate) * total(jnp.sum(row_lanes, axis=1), "col", n_col) / F
    by_row = jnp.full((1, 128), jnp.sum(weighted / row_new) / 128)
    by_col = jnp.sum(squared * (1.0 / row_new)[:, None], axis=0, keepdims=True)
    sums = over_rows(jnp.concatenate([col_sum, by_col, by_row], axis=1))[0]
    count = high - low
    col_new.append(held + (1.0 - decay_rate) * sums[:count] / D)
    update_total = jnp.sum(sums[count : 2 * count] / col_new[-1]) + jnp.sum(sums[2 * count :])
    update_total = total(update_total.reshape(1, 1), "col", n_col)[0, 0]
    col_new = jnp.concatenate(col_new)
    clip_factor = jnp.maximum(1.0, jnp.sqrt(update_total / (D * F)))
    new_weight, clipped = weight_step(
        relative, 1.0 / clip_factor, lax.rsqrt(row_new), lax.rsqrt(col_new), weight, grad
    )
    return (new_weight, clipped, row_new, col_new)


def solution(mesh):
    placed = (
        P(("dp", "col"), "row"),
        P(("dp", "row"), "col"),
        P(("row", "dp"), "col"),
        P(("row", "dp")),
        P("col"),
    )
    sizes = (mesh.shape["dp"], mesh.shape["row"], mesh.shape["col"])
    return jax.shard_map(
        functools.partial(body, sizes),
        mesh=mesh,
        in_specs=placed,
        out_specs=(P(("row", "dp"), "col"), P(("row", "dp"), "col"), P(("row", "dp")), P("col")),
        check_vma=False,
    )
```
